512 devices in a mesh: seq: 128 (over x, y_hi, z), head: 4 (over y_lo, core).
Axes of the slice: x: 4, y: 8 (y_hi: 4, y_lo: 2; y = y_hi * 2 + y_lo), z: 8, core: 2. Of those that a mesh axis runs over, the one named last changes fastest.
Arguments:
- queries: bfloat16 [32768, 16, 128], P('seq', 'head'), may hold values from -4.5 to 4.5
- keys: bfloat16 [32768, 16, 128], P('seq', 'head'), may hold values from -4.5 to 4.5
- values: bfloat16 [32768, 16, 128], P('seq', 'head'), may hold values from -6 to 6
- out_weight: bfloat16 [2048, 2048], P('head'), may hold values from -0.75 to 0.75
- cotangent: bfloat16 [32768, 2048], P(('seq', 'head')), may hold values from -6 to 6
- doc_lengths: int32 [128], replicated, may hold values from 1 to 1024, 32768 in all
Outputs:
- projected: bfloat16 [32768, 2048], P(('seq', 'head'))
- grad_queries: bfloat16 [32768, 16, 128], P('seq', 'head')
- grad_keys: bfloat16 [32768, 16, 128], P('seq', 'head')
- grad_values: bfloat16 [32768, 16, 128], P('seq', 'head')
The draws below stay inside these ranges and needn't reach their ends.
Inputs may be any that keep to these rules, and one draw needn't show every extreme that they name: `doc_lengths`: lengths of the packed documents in order; they sum to 32768 and the longest is exactly 1024.
All inputs are finite; a program needn't handle non-finite values.
Results may differ from the reference program's by a relative error of at most 0.024.
Values may be sent and summed in bfloat16 or wider, within the bound.
A program may use at most 64 MiB of HBM per device.

```python
import math
import jax
import jax.numpy as jnp
import numpy as np
from jax import lax

TOK_DEV = 256
HD = 128
HEAD_DEV = 4
D = 2048
SPAN = 4
HEADS = 16
SEQ = 32768
DOCS = 128
N_SEQ = 128
N_HEAD = 4


def draw_queries(key, part):
    own_key = jax.random.fold_in(key, 1)
    return jnp.clip(jax.random.normal(own_key, (SEQ, HEADS, HD)), -4.5, 4.5).astype(jnp.bfloat16)


def draw_keys(key, part):
    own_key = jax.random.fold_in(key, 2)
    return jnp.clip(jax.random.normal(own_key, (SEQ, HEADS, HD)), -4.5, 4.5).astype(jnp.bfloat16)


def shard_levels(key, dims, pieces, low, largest):
    gain = 1.0
    for position, shards_of in pieces:
        draws = jax.random.uniform(jax.random.fold_in(jax.random.fold_in(key, 6), position), (shards_of,), jnp.float32, low / len(pieces), largest / len(pieces))
        gain = gain * jnp.repeat(jnp.exp(draws), dims[position] // shards_of).reshape((-1,) + (1,) * (len(dims) - 1 - position))
    return gain


def profile(count, total, limit, slope):
    loads = [(1 << 20) // math.isqrt(standing ** slope) + 1 for standing in range(2, count + 1)]
    rest, given = total - limit - (count - 1), [1] * (count - 1)
    while rest > 0:
        candidates = [i for i in range(count - 1) if given[i] < limit]
        whole, budget = sum([loads[i] for i in candidates]), rest
        for i in candidates:
            more = min(limit - given[i], max(1, budget * loads[i] // whole), rest)
            given[i] = given[i] + more
            rest = rest - more
    return np.array([limit] + given)


def ragged(key, amount, total, bound, slope):
    if amount == 2:
        one = jax.random.randint(key, (), max(1, total - bound), min(bound, total - 1) + 1)
        return jnp.stack([one, total - one])
    tallies = jnp.asarray(profile(amount, total, bound, slope), jnp.int32)
    couples = (amount - 1) // 2
    donor, sink = tallies[1:1 + 2 * couples:2], tallies[2:2 + 2 * couples:2]
    margin = jnp.minimum(donor - 1, bound - sink)
    passed = jax.random.randint(jax.random.fold_in(key, 1), (couples,), 0, 1 << 20) % (margin + 1)
    tallies = tallies.at[1:1 + 2 * couples:2].set(donor - passed).at[2:2 + 2 * couples:2].set(sink + passed)
    return tallies[jax.random.permutation(jax.random.fold_in(key, 2), amount)]


def centred(key, extent, width, most, shards=(), kind=jnp.bfloat16):
    drawn = jax.random.normal(key, extent, jnp.float32) * width
    if len(shards) > 0:
        drawn = shard_levels(key, extent, shards, -0.22, 0.18) * drawn
    return jnp.clip(drawn, min=-most, max=most).astype(kind)


def setup_inputs(seed: int = 0) -> dict:
    seeds = jax.random.split(jax.random.key(seed), 7)
    queries = draw_queries(jax.random.fold_in(seeds[6], 71), 0)
    keys = draw_keys(jax.random.fold_in(seeds[6], 71), 0)
    values = centred(seeds[2], (SEQ, HEADS, HD), 1.0, 6.0, ((0, 128), (1, 4)))
    out_weight = centred(seeds[3], (HEADS * HD, D), 0.125, 0.75, ((0, 4),))
    cotangent = centred(seeds[4], (SEQ, D), 1.0, 6.0, ((0, 512),))
    doc_lengths = ragged(seeds[5], DOCS, SEQ, SPAN * TOK_DEV, 2).astype(jnp.int32)
    return dict(queries=queries, keys=keys, values=values, out_weight=out_weight, cotangent=cotangent, doc_lengths=doc_lengths)


NEG = -1.0e30


def doc_index(positions, doc_lengths):
    doc_ends = jnp.cumsum(doc_lengths).astype(jnp.int32)
    return jnp.sum((doc_ends[None, :] <= positions[:, None]).astype(jnp.int32), axis=1)


def visible_pairs(q_pos, k_pos, doc_lengths):
    inside = (k_pos[None, :] >= 0) & (k_pos[None, :] <= q_pos[:, None])
    return inside & (doc_index(q_pos, doc_lengths)[:, None] == doc_index(k_pos, doc_lengths)[None, :])


def raw_scores(q_part, k_part, visible):
    factor = float(HD) ** -0.5
    product = jnp.einsum("qhd,khd->hqk", q_part.astype(jnp.float32), k_part.astype(jnp.float32)) * factor
    return jnp.where(visible[None], product, NEG)


def low_round(values_in):
    return lax.optimization_barrier(values_in.astype(jnp.bfloat16)).astype(jnp.float32)


def reference(queries, keys, values, out_weight, cotangent, doc_lengths):
    factor = float(HD) ** -0.5
    window = (SPAN + 1) * TOK_DEV
    reach = SPAN * TOK_DEV
    front = jnp.zeros((reach, HEADS, HD), jnp.bfloat16)
    keys_padded = jnp.concatenate([front, keys], axis=0)
    values_padded = jnp.concatenate([front, values], axis=0)
    blocks = jnp.arange(N_SEQ, dtype=jnp.int32)

    def forward_block(block):
        first_row = block * TOK_DEV
        q_part = lax.dynamic_slice_in_dim(queries, first_row, TOK_DEV, 0)
        k_part = lax.dynamic_slice_in_dim(keys_padded, first_row, window, 0)
        v_part = lax.dynamic_slice_in_dim(values_padded, first_row, window, 0)
        q_pos = first_row + jnp.arange(TOK_DEV, dtype=jnp.int32)
        k_pos = first_row - reach + jnp.arange(window, dtype=jnp.int32)
        scored = raw_scores(q_part, k_part, visible_pairs(q_pos, k_pos, doc_lengths))
        row_max = jnp.max(scored, axis=-1)
        weights = jnp.exp(scored - row_max[..., None])
        row_total = jnp.sum(weights, axis=-1)
        weighted = jnp.einsum("hqk,khd->qhd", low_round(weights), v_part.astype(jnp.float32))
        attended = (weighted / jnp.transpose(row_total)[:, :, None]).astype(jnp.bfloat16)
        return attended, jnp.transpose(row_max + jnp.log(row_total))

    attended, logsum = lax.map(forward_block, blocks)
    attended = attended.reshape(SEQ, HEADS, HD)
    logsum = logsum.reshape(SEQ, HEADS)

    span_cols = HEAD_DEV * HD
    flat_heads = attended.reshape(SEQ, HEADS * HD)
    summed = jnp.zeros((SEQ, D), jnp.float32)
    for group_id in range(N_HEAD):
        lower = group_id * span_cols
        term = jnp.dot(flat_heads[:, lower:lower + span_cols], out_weight[lower:lower + span_cols], preferred_element_type=jnp.float32)
        summed = summed + low_round(term)
    projected = summed.astype(jnp.bfloat16)

    d_attended = jnp.dot(cotangent, out_weight.T, preferred_element_type=jnp.float32).astype(jnp.bfloat16)
    d_attended = d_attended.reshape(SEQ, HEADS, HD)
    deltas = jnp.sum(d_attended.astype(jnp.float32) * attended.astype(jnp.float32), axis=-1)

    def query_grads(block):
        first_row = block * TOK_DEV
        q_part = lax.dynamic_slice_in_dim(queries, first_row, TOK_DEV, 0)
        grad_part = lax.dynamic_slice_in_dim(d_attended, first_row, TOK_DEV, 0)
        lse_part = lax.dynamic_slice_in_dim(logsum, first_row, TOK_DEV, 0)
        delta_part = lax.dynamic_slice_in_dim(deltas, first_row, TOK_DEV, 0)
        k_part = lax.dynamic_slice_in_dim(keys_padded, first_row, window, 0)
        v_part = lax.dynamic_slice_in_dim(values_padded, first_row, window, 0)
        q_pos = first_row + jnp.arange(TOK_DEV, dtype=jnp.int32)
        k_pos = first_row - reach + jnp.arange(window, dtype=jnp.int32)
        scored = raw_scores(q_part, k_part, visible_pairs(q_pos, k_pos, doc_lengths))
        probs = jnp.exp(scored - jnp.transpose(lse_part)[:, :, None])
        grad_probs = jnp.einsum("qhd,khd->hqk", grad_part.astype(jnp.float32), v_part.astype(jnp.float32))
        grad_scores = low_round(probs * (grad_probs - jnp.transpose(delta_part)[:, :, None]))
        grad_q = jnp.einsum("hqk,khd->qhd", grad_scores, k_part.astype(jnp.float32)) * factor
        return grad_q.astype(jnp.bfloat16)

    grad_queries = lax.map(query_grads, blocks).reshape(SEQ, HEADS, HD)

    tail = jnp.zeros((reach, HEADS, HD), jnp.bfloat16)
    tail_stats = jnp.zeros((reach, HEADS), jnp.float32)
    queries_padded = jnp.concatenate([queries, tail], axis=0)
    grads_padded = jnp.concatenate([d_attended, tail], axis=0)
    logsum_padded = jnp.concatenate([logsum, tail_stats], axis=0)
    deltas_padded = jnp.concatenate([deltas, tail_stats], axis=0)

    def key_grads(block):
        first_row = block * TOK_DEV
        k_part = lax.dynamic_slice_in_dim(keys, first_row, TOK_DEV, 0)
        v_part = lax.dynamic_slice_in_dim(values, first_row, TOK_DEV, 0)
        q_part = lax.dynamic_slice_in_dim(queries_padded, first_row, window, 0)
        grad_part = lax.dynamic_slice_in_dim(grads_padded, first_row, window, 0)
        lse_part = lax.dynamic_slice_in_dim(logsum_padded, first_row, window, 0)
        delta_part = lax.dynamic_slice_in_dim(deltas_padded, first_row, window, 0)
        q_pos = first_row + jnp.arange(window, dtype=jnp.int32)
        k_pos = first_row + jnp.arange(TOK_DEV, dtype=jnp.int32)
        visible = visible_pairs(q_pos, k_pos, doc_lengths) & (q_pos < SEQ)[:, None]
        scored = raw_scores(q_part, k_part, visible)
        probs = jnp.exp(scored - jnp.transpose(lse_part)[:, :, None])
        grad_v = jnp.einsum("hqk,qhd->khd", low_round(probs), grad_part.astype(jnp.float32))
        grad_probs = jnp.einsum("qhd,khd->hqk", grad_part.astype(jnp.float32), v_part.astype(jnp.float32))
        grad_scores = low_round(probs * (grad_probs - jnp.transpose(delta_part)[:, :, None]))
        grad_k = jnp.einsum("hqk,qhd->khd", grad_scores, q_part.astype(jnp.float32)) * factor
        return grad_k.astype(jnp.bfloat16), grad_v.astype(jnp.bfloat16)

    grad_keys, grad_values = lax.map(key_grads, blocks)
    grad_keys = grad_keys.reshape(SEQ, HEADS, HD)
    grad_values = grad_values.reshape(SEQ, HEADS, HD)
    return projected, grad_queries, grad_keys, grad_values
```

```python
import functools
import math

import jax
import jax.numpy as jnp
from jax import lax
from jax.experimental import pallas as pl
from jax.experimental.pallas import tpu as pltpu
from jax.sharding import PartitionSpec as P

MESH = pl.DeviceIdType.MESH
T = 256
HD = 128
NB = 4
RING = 8
WIN = 5
D = 2048
ROWS = 64
NEG = -1e30
FACTOR = HD ** (-0.5)
SCALE = FACTOR * math.log2(math.e)
BF = jnp.bfloat16
F32 = jnp.float32


def nt(a, b):
    return lax.dot_general(a, b, (((1,), (1,)), ((), ())), preferred_element_type=F32)


def nn(a, b):
    return jnp.dot(a, b, preferred_element_type=F32)


def fold(x, op):
    parts = [x[r : r + 8] for r in range(0, x.shape[0], 8)]
    while len(parts) > 1:
        parts = [
            op(parts[j], parts[j + 1]) if j + 1 < len(parts) else parts[j]
            for j in range(0, len(parts), 2)
        ]
    return parts[0]


def kernel(
    seq_size,
    q_ref,
    k_ref,
    v_ref,
    w_hbm,
    cot_ref,
    len_ref,
    proj_ref,
    dq_ref,
    dk_ref,
    dv_ref,
    kbuf,
    vbuf,
    qbuf,
    dobuf,
    kT,
    vT,
    cotbuf,
    wbuf,
    doloc,
    sbuf,
    pbuf,
    oT,
    linv,
    lo,
    dkacc,
    dvacc,
    hko,
    hvo,
    hki,
    hvi,
    oout,
    dqout,
    dkout,
    dvout,
    oin,
    pa_out,
    pa_in,
    pb_out,
    pb_in,
    in_send,
    in_recv,
    halo_send,
    halo_recv,
    cot_send,
    cot_recv,
    out_send,
    out_recv,
    hg_send,
    hg_recv,
    pr_send,
    pr_recv,
    w_sem,
):
    s = lax.axis_index("seq")
    h = lax.axis_index("head")
    z = lax.rem(s, RING)
    base = s - z
    c = lax.rem(h, 2)
    yl = h // 2
    half = z // NB
    zi = lax.rem(z, NB)
    sib = (s, h + 1 - 2 * c)
    across = (s, lax.rem(h + 2, 4))
    h_next = (lax.rem(s + RING * c, seq_size), h + 1 - 2 * c)
    h_prev = (lax.rem(s + seq_size - RING * (1 - c), seq_size), h + 1 - 2 * c)
    ring_adj = (lax.rem(s + seq_size + RING * (2 * c - 1), seq_size), h + 1 - 2 * c)

    def peer(i):
        return (base + NB * c + i, h - c + half)

    def is_self(i):
        return (c == half) & (zi == i)

    barrier = pltpu.get_barrier_semaphore()
    for dev in (sib, across, ring_adj):
        pl.semaphore_signal(barrier, inc=1, device_id=dev, device_id_type=MESH)
    for i in range(NB):

        @pl.when(jnp.logical_not(is_self(i)))
        def _():
            pl.semaphore_signal(barrier, inc=1, device_id=peer(i), device_id_type=MESH)

    @pl.when(c == half)
    def _():
        pl.semaphore_wait(barrier, 6)

    @pl.when(c != half)
    def _():
        pl.semaphore_wait(barrier, 7)

    def remote(src, dst, ssem, rsem, dev):
        return pltpu.make_async_remote_copy(
            src_ref=src, dst_ref=dst, send_sem=ssem, recv_sem=rsem, device_id=dev, device_id_type=MESH
        )

    def rows(i, n=T):
        return pl.ds(pl.multiple_of(i * n, n), n)

    def send_peer(i, src, dst, ssem, rsem):
        @pl.when(jnp.logical_not(is_self(i)))
        def _():
            remote(src, dst, ssem, rsem, peer(i)).start()

        @pl.when(is_self(i))
        def _():
            pltpu.make_async_copy(src, dst, rsem).start()

    def sent_peer(i, src, dst, ssem, rsem):
        @pl.when(jnp.logical_not(is_self(i)))
        def _():
            remote(src, dst, ssem, rsem, peer(i)).wait_send()

    def arrived(dst, rsem):
        pltpu.make_async_copy(dst, dst, rsem).wait()

    w_copy = pltpu.make_async_copy(w_hbm, wbuf, w_sem)
    w_copy.start()

    def in_args(a, i):
        src = (k_ref, v_ref, q_ref, doloc)[a].at[:, pl.ds(i * HD, HD)]
        if a < 2:
            dst = (kbuf, vbuf)[a].at[rows(NB + zi)]
        else:
            dst = (qbuf, dobuf)[a - 2].at[rows(zi)]
        return i, src, dst, in_send.at[a, i], in_recv.at[a, zi]

    def in_dst(a, j):
        if a < 2:
            return (kbuf, vbuf)[a].at[rows(NB + j)], in_recv.at[a, j]
        return (qbuf, dobuf)[a - 2].at[rows(j)], in_recv.at[a, j]

    for i in range(NB):
        send_peer(*in_args(0, i))
    def cot_rows(g):
        return cotbuf.at[rows(g, ROWS)]

    cot_x = remote(cot_ref, cot_rows(h), cot_send.at[0], cot_recv.at[0], across)
    cot_s = remote(cot_ref, cot_rows(h), cot_send.at[1], cot_recv.at[1], sib)
    cot_x.start()
    cot_s.start()
    for a in (1, 2):
        for i in range(NB):
            send_peer(*in_args(a, i))
    cotbuf[rows(h, ROWS), :] = cot_ref[...]

    lens = len_ref[...].astype(F32)
    d_i = lax.broadcasted_iota(jnp.int32, (128, 128), 0)
    e_i = lax.broadcasted_iota(jnp.int32, (128, 128), 1)
    starts = jnp.sum(jnp.where(e_i < d_i, jnp.broadcast_to(lens, (128, 128)), 0.0), axis=1, keepdims=True)
    first = (base + NB * c) * T
    pos = (first + lax.broadcasted_iota(jnp.int32, (128, NB * T), 1)).astype(F32)
    started = jnp.where(jnp.broadcast_to(starts, (128, NB * T)) <= pos, starts, 0.0)
    low = jnp.max(started, axis=0, keepdims=True).astype(jnp.int32) - (first - NB * T)
    lo[...] = jnp.broadcast_to(low, (8, NB * T))
    dkacc[...] = jnp.zeros_like(dkacc)
    dvacc[...] = jnp.zeros_like(dvacc)

    def halo(a, j):
        buf = (kbuf, vbuf)[a]
        return remote(buf.at[rows(NB + j)], buf.at[rows(j)], halo_send.at[a, j], halo_recv.at[a, j], h_next)

    cot_f = remote(
        cot_rows(across[1]), cot_rows(across[1]), cot_send.at[2], cot_recv.at[2], sib
    )
    for j in range(NB):
        arrived(*in_dst(0, j))
        halo(0, j).start()
    arrived(cot_rows(across[1]), cot_recv.at[0])
    cot_f.start()
    for j in range(NB):
        arrived(*in_dst(1, j))
        halo(1, j).start()

    w_copy.wait()
    arrived(cot_rows(sib[1]), cot_recv.at[1])
    arrived(cot_rows(lax.rem(sib[1] + 2, 4)), cot_recv.at[2])
    doloc[...] = nt(cotbuf[...], wbuf[...]).astype(BF)
    for i in range(NB):
        send_peer(*in_args(3, i))

    for a in range(2):
        for j in range(NB):
            arrived((kbuf, vbuf)[a].at[rows(j)], halo_recv.at[a, j])
    for b in range(2 * NB):
        kT[:, b * T : (b + 1) * T] = kbuf[b * T : (b + 1) * T, :].T
        vT[:, b * T : (b + 1) * T] = vbuf[b * T : (b + 1) * T, :].T
    for j in range(NB):
        arrived(*in_dst(2, j))

    r_i = lax.broadcasted_iota(jnp.int32, (T, T), 0)
    t_i = lax.broadcasted_iota(jnp.int32, (T, T), 1)

    def out_args(a, i):
        src = (oout, dqout, dvout, dkout)[a].at[rows(i)]
        dst = (oin, dq_ref, dv_ref, dk_ref)[a].at[:, rows(zi, HD)]
        return i, src, dst, out_send.at[a, i], out_recv.at[a, zi]

    def out_dst(a, j):
        return (oin, dq_ref, dv_ref, dk_ref)[a].at[:, rows(j, HD)], out_recv.at[a, j]

    @pl.loop(0, NB)
    def _(i):
        q = qbuf[rows(i), :]
        low = lo[0:1, rows(i)] - i * T
        top = None
        for b in range(WIN):
            scores = nt(kbuf[rows(i + b), :], q)
            seen = r_i + b * T >= low
            if b == WIN - 1:
                seen = seen & (r_i <= t_i)
            scores = jnp.where(seen, scores, NEG)
            sbuf[b * T : (b + 1) * T, :] = scores
            part = fold(scores, jnp.maximum)
            top = part if top is None else jnp.maximum(top, part)
        top = jnp.max(top, axis=0, keepdims=True) * SCALE
        total = None
        att = None
        for b in range(WIN):
            p = jnp.exp2(sbuf[b * T : (b + 1) * T, :] * SCALE - top)
            part = fold(p, jnp.add)
            total = part if total is None else total + part
            pb = p.astype(BF)
            pbuf[rows(i * WIN + b), :] = pb
            term = nn(vT[:, rows(i + b)], pb)
            att = term if att is None else att + term
        inv = 1.0 / jnp.sum(total, axis=0, keepdims=True)
        linv[rows(i, 8), :] = jnp.broadcast_to(inv, (8, T))
        att = (att * inv).astype(BF)
        oT[rows(i, HD), :] = att
        oout[rows(i), :] = att.T
        send_peer(*out_args(0, i))

    for j in range(NB):
        arrived(*in_dst(3, j))

    def back(a, u):
        src, dst = ((hvo, hvi), (hko, hki))[a]
        return remote(src.at[rows(u)], dst.at[rows(u)], hg_send.at[a, u], hg_recv.at[a, u], h_prev)

    @pl.loop(0, NB)
    def _(i):
        q = qbuf[rows(i), :]
        inv = linv[rows(i, 8), :][0:1]
        doT = dobuf[rows(i), :].astype(F32).T * inv
        delta = jnp.sum(doT * oT[rows(i, HD), :].astype(F32), axis=0, keepdims=True)
        doT = doT.astype(BF)
        do = doT.T
        gq = None
        for b in range(WIN):
            pb = pbuf[rows(i * WIN + b), :]
            dvacc[rows(i + b), :] += nn(pb, do)
            dp = nn(vbuf[rows(i + b), :], doT)
            ds = (pb.astype(F32) * (dp - delta)).astype(BF)
            term = nn(kT[:, rows(i + b)], ds)
            gq = term if gq is None else gq + term
            dkacc[rows(i + b), :] += nn(ds, q)
        dqout[rows(i), :] = (gq * FACTOR).astype(BF).T
        send_peer(*out_args(1, i))
        hvo[rows(i), :] = dvacc[rows(i), :].astype(BF)
        back(0, i).start()
        hko[rows(i), :] = dkacc[rows(i), :].astype(BF)
        back(1, i).start()

    for j in range(NB):
        arrived(*out_dst(0, j))

    def o_rows(first_row):
        return oin[rows(first_row, ROWS), :]

    other = jnp.concatenate([o_rows(1 - c), o_rows(3 - c)], axis=0)
    pa_out[...] = nn(other, wbuf[...]).astype(BF)
    pr_a = remote(pa_out, pa_in, pr_send.at[0], pr_recv.at[0], sib)
    pr_a.start()

    for u in range(NB):
        arrived(hvi.at[rows(u)], hg_recv.at[0, u])
        dvout[rows(u), :] = (dvacc[rows(NB + u), :] + hvi[rows(u), :].astype(F32)).astype(BF)
        send_peer(*out_args(2, u))

    far = nn(o_rows(c + 2 * (1 - yl)), wbuf[...])
    arrived(pa_in, pr_recv.at[0])
    pb_out[...] = (far + pa_in[rows(1 - yl, ROWS), :].astype(F32)).astype(BF)
    pr_b = remote(pb_out, pb_in, pr_send.at[1], pr_recv.at[1], across)
    pr_b.start()
    near = nn(o_rows(h), wbuf[...]) + pa_in[rows(yl, ROWS), :].astype(F32)

    for u in range(NB):
        arrived(hki.at[rows(u)], hg_recv.at[1, u])
        own = dkacc[rows(NB + u), :] + hki[rows(u), :].astype(F32)
        dkout[rows(u), :] = (own * FACTOR).astype(BF)
        send_peer(*out_args(3, u))

    arrived(pb_in, pr_recv.at[1])
    proj_ref[...] = (near + pb_in[...].astype(F32)).astype(BF)

    for a in range(1, 4):
        for j in range(NB):
            arrived(*out_dst(a, j))

    for a in range(4):
        for i in range(NB):
            sent_peer(*in_args(a, i))
            sent_peer(*out_args(a, i))
    for a in range(2):
        for j in range(NB):
            halo(a, j).wait_send()
            back(a, j).wait_send()
    for copy in (cot_x, cot_s, cot_f, pr_a, pr_b):
        copy.wait_send()


def per_device(seq_size, queries, keys, values, out_weight, cotangent, doc_lengths):
    flat = [x.reshape(T, NB * HD) for x in (queries, keys, values)]
    vmem = pl.BlockSpec(memory_space=pltpu.VMEM)

    def sc(*shape, dtype=BF):
        return pltpu.VMEM(shape, dtype)

    dma = pltpu.SemaphoreType.DMA
    half = NB * T
    proj, dq, dk, dv = pl.pallas_call(
        functools.partial(kernel, seq_size),
        out_shape=[jax.ShapeDtypeStruct((ROWS, D), BF)]
        + [jax.ShapeDtypeStruct((T, NB * HD), BF)] * 3,
        in_specs=[vmem, vmem, vmem, pl.BlockSpec(memory_space=pl.ANY), vmem, vmem],
        out_specs=[vmem] * 4,
        scratch_shapes=[
            sc(2 * half, HD),
            sc(2 * half, HD),
            sc(half, HD),
            sc(half, HD),
            sc(HD, 2 * half),
            sc(HD, 2 * half),
            sc(T, D),
            sc(NB * HD, D),
            sc(T, NB * HD),
            sc(WIN * T, T, dtype=F32),
            sc(NB * WIN * T, T),
            sc(NB * HD, T),
            sc(NB * 8, T, dtype=F32),
            sc(8, half, dtype=jnp.int32),
            sc(2 * half, HD, dtype=F32),
            sc(2 * half, HD, dtype=F32),
            sc(half, HD),
            sc(half, HD),
            sc(half, HD),
            sc(half, HD),
            sc(half, HD),
            sc(half, HD),
            sc(half, HD),
            sc(half, HD),
            sc(T, NB * HD),
            sc(2 * ROWS, D),
            sc(2 * ROWS, D),
            sc(ROWS, D),
            sc(ROWS, D),
            dma((4, NB)),
            dma((4, NB)),
            dma((2, NB)),
            dma((2, NB)),
            dma((3,)),
            dma((3,)),
            dma((4, NB)),
            dma((4, NB)),
            dma((2, NB)),
            dma((2, NB)),
            dma((2,)),
            dma((2,)),
            dma(()),
        ],
        compiler_params=pltpu.CompilerParams(
            collective_id=0, has_side_effects=True, vmem_limit_bytes=48 * 1024 * 1024
        ),
        name="ring_attention",
    )(*flat, out_weight, cotangent, doc_lengths.reshape(1, -1))
    return (proj,) + tuple(x.reshape(T, NB, HD) for x in (dq, dk, dv))


def solution(mesh):
    seq_head = P("seq", "head", None)
    rows = P(("seq", "head"), None)
    return jax.shard_map(
        functools.partial(per_device, mesh.shape["seq"]),
        mesh=mesh,
        in_specs=(seq_head, seq_head, seq_head, P("head", None), rows, P()),
        out_specs=(rows, seq_head, seq_head, seq_head),
        check_vma=False,
    )
```

```python
import functools
import math

import jax
import jax.numpy as jnp
from jax import lax
from jax.experimental import pallas as pl
from jax.experimental.pallas import tpu as pltpu
from jax.sharding import PartitionSpec as P

MESH = pl.DeviceIdType.MESH
T = 256
HD = 128
NB = 4
RING = 8
WIN = 5
D = 2048
ROWS = 64
NEG = -1e30
FACTOR = HD ** (-0.5)
SCALE = FACTOR * math.log2(math.e)
BF = jnp.bfloat16
F32 = jnp.float32


def nt(a, b):
    return lax.dot_general(a, b, (((1,), (1,)), ((), ())), preferred_element_type=F32)


def nn(a, b):
    return jnp.dot(a, b, preferred_element_type=F32)


def fold(x, op):
    parts = [x[r : r + 8] for r in range(0, x.shape[0], 8)]
    while len(parts) > 1:
        parts = [
            op(parts[j], parts[j + 1]) if j + 1 < len(parts) else parts[j]
            for j in range(0, len(parts), 2)
        ]
    return parts[0]


def kernel(
    seq_size,
    q_hbm,
    k_hbm,
    v_hbm,
    w_hbm,
    cot_hbm,
    len_hbm,
    proj_ref,
    dq_ref,
    dk_ref,
    dv_ref,
    kbuf,
    vbuf,
    qbuf,
    dobuf,
    kT,
    vT,
    cotbuf,
    wbuf,
    doloc,
    sbuf,
    pbuf,
    oT,
    linv,
    lo,
    dkacc,
    dvacc,
    hko,
    hvo,
    hki,
    hvi,
    oout,
    dqout,
    dkout,
    dvout,
    k_ref,
    v_ref,
    q_ref,
    cot_ref,
    len_ref,
    kloc,
    vloc,
    qloc,
    oin,
    dqin,
    dvin,
    dkin,
    pa_out,
    pa_in,
    pb_out,
    pb_in,
    in_send,
    in_recv,
    halo_send,
    halo_recv,
    cot_send,
    cot_recv,
    out_send,
    out_recv,
    hg_send,
    hg_recv,
    pr_send,
    pr_recv,
    w_sem,
):
    s = lax.axis_index("seq")
    h = lax.axis_index("head")
    z = lax.rem(s, RING)
    base = s - z
    c = lax.rem(h, 2)
    yl = h // 2
    half = z // NB
    zi = lax.rem(z, NB)
    sib = (s, h + 1 - 2 * c)
    across = (s, lax.rem(h + 2, 4))
    h_next = (lax.rem(s + RING * c, seq_size), h + 1 - 2 * c)
    h_prev = (lax.rem(s + seq_size - RING * (1 - c), seq_size), h + 1 - 2 * c)
    ring_adj = (lax.rem(s + seq_size + RING * (2 * c - 1), seq_size), h + 1 - 2 * c)

    def peer(i):
        return (base + NB * c + i, h - c + half)

    def is_self(i):
        return (c == half) & (zi == i)

    loads = [
        pltpu.make_async_copy(src, dst, w_sem.at[n])
        for n, (src, dst) in enumerate(
            (
                (k_hbm, k_ref),
                (v_hbm, v_ref),
                (q_hbm, q_ref),
                (cot_hbm, cot_ref),
                (len_hbm, len_ref),
                (w_hbm, wbuf),
            )
        )
    ]
    for copy in loads:
        copy.start()

    barrier = pltpu.get_barrier_semaphore()
    for dev in (sib, across, ring_adj):
        pl.semaphore_signal(barrier, inc=1, device_id=dev, device_id_type=MESH)
    for i in range(NB):

        @pl.when(jnp.logical_not(is_self(i)))
        def _():
            pl.semaphore_signal(barrier, inc=1, device_id=peer(i), device_id_type=MESH)

    def remote(src, dst, ssem, rsem, dev):
        return pltpu.make_async_remote_copy(
            src_ref=src, dst_ref=dst, send_sem=ssem, recv_sem=rsem, device_id=dev, device_id_type=MESH
        )

    def rows(i, n=T):
        return pl.ds(pl.multiple_of(i * n, n), n)

    def send_peer(i, src, dst, ssem, rsem):
        @pl.when(jnp.logical_not(is_self(i)))
        def _():
            remote(src, dst, ssem, rsem, peer(i)).start()

        @pl.when(is_self(i))
        def _():
            pltpu.make_async_copy(src, dst, rsem).start()

    def sent_peer(i, src, dst, ssem, rsem):
        @pl.when(jnp.logical_not(is_self(i)))
        def _():
            remote(src, dst, ssem, rsem, peer(i)).wait_send()

    def arrived(dst, rsem):
        pltpu.make_async_copy(dst, dst, rsem).wait()

    def split(src, dst):
        for i in range(NB):
            dst[i * T : (i + 1) * T, :] = src[:, i, :]


    def in_args(a, i):
        src = (kloc, vloc, qloc, doloc)[a].at[rows(i)]
        if a < 2:
            dst = (kbuf, vbuf)[a].at[rows(NB + zi)]
        else:
            dst = (qbuf, dobuf)[a - 2].at[rows(zi)]
        return i, src, dst, in_send.at[a, i], in_recv.at[a, zi]

    def in_dst(a, j):
        if a < 2:
            return (kbuf, vbuf)[a].at[rows(NB + j)], in_recv.at[a, j]
        return (qbuf, dobuf)[a - 2].at[rows(j)], in_recv.at[a, j]

    loads[0].wait()
    split(k_ref, kloc)
    loads[3].wait()
    @pl.when(c == half)
    def _():
        pl.semaphore_wait(barrier, 6)

    @pl.when(c != half)
    def _():
        pl.semaphore_wait(barrier, 7)

    for i in range(NB):
        send_peer(*in_args(0, i))
    def cot_rows(g):
        return cotbuf.at[rows(g, ROWS)]

    cot_x = remote(cot_ref, cot_rows(h), cot_send.at[0], cot_recv.at[0], across)
    cot_s = remote(cot_ref, cot_rows(h), cot_send.at[1], cot_recv.at[1], sib)
    cot_x.start()
    cot_s.start()
    for a in (1, 2):
        loads[a].wait()
        split((k_ref, v_ref, q_ref)[a], (kloc, vloc, qloc)[a])
        for i in range(NB):
            send_peer(*in_args(a, i))
    cotbuf[rows(h, ROWS), :] = cot_ref[...]

    loads[4].wait()
    lens = len_ref[...].astype(F32)
    d_i = lax.broadcasted_iota(jnp.int32, (128, 128), 0)
    e_i = lax.broadcasted_iota(jnp.int32, (128, 128), 1)
    starts = jnp.sum(jnp.where(e_i < d_i, jnp.broadcast_to(lens, (128, 128)), 0.0), axis=1, keepdims=True)
    first = (base + NB * c) * T
    pos = (first + lax.broadcasted_iota(jnp.int32, (128, NB * T), 1)).astype(F32)
    started = jnp.where(jnp.broadcast_to(starts, (128, NB * T)) <= pos, starts, 0.0)
    low = jnp.max(started, axis=0, keepdims=True).astype(jnp.int32) - (first - NB * T)
    lo[...] = jnp.broadcast_to(low, (8, NB * T))
    dkacc[...] = jnp.zeros_like(dkacc)
    dvacc[...] = jnp.zeros_like(dvacc)

    def halo(a, j):
        buf = (kbuf, vbuf)[a]
        return remote(buf.at[rows(NB + j)], buf.at[rows(j)], halo_send.at[a, j], halo_recv.at[a, j], h_next)

    cot_f = remote(
        cot_rows(across[1]), cot_rows(across[1]), cot_send.at[2], cot_recv.at[2], sib
    )
    for j in range(NB):
        arrived(*in_dst(0, j))
        halo(0, j).start()
    arrived(cot_rows(across[1]), cot_recv.at[0])
    cot_f.start()
    for j in range(NB):
        arrived(*in_dst(1, j))
        halo(1, j).start()

    loads[5].wait()
    arrived(cot_rows(sib[1]), cot_recv.at[1])
    arrived(cot_rows(lax.rem(sib[1] + 2, 4)), cot_recv.at[2])
    d_att = nt(cotbuf[...], wbuf[...]).astype(BF)
    for i in range(NB):
        doloc[i * T : (i + 1) * T, :] = d_att[:, i * HD : (i + 1) * HD]
        send_peer(*in_args(3, i))

    for a in range(2):
        for j in range(NB):
            arrived((kbuf, vbuf)[a].at[rows(j)], halo_recv.at[a, j])
    for b in range(2 * NB):
        kT[:, b * T : (b + 1) * T] = kbuf[b * T : (b + 1) * T, :].T
        vT[:, b * T : (b + 1) * T] = vbuf[b * T : (b + 1) * T, :].T
    for j in range(NB):
        arrived(*in_dst(2, j))

    r_i = lax.broadcasted_iota(jnp.int32, (T, T), 0)
    t_i = lax.broadcasted_iota(jnp.int32, (T, T), 1)

    def out_args(a, i):
        src = (oout, dqout, dvout, dkout)[a].at[rows(i)]
        dst = (oin, dqin, dvin, dkin)[a].at[rows(zi)]
        return i, src, dst, out_send.at[a, i], out_recv.at[a, zi]

    def out_dst(a, j):
        return (oin, dqin, dvin, dkin)[a].at[rows(j)], out_recv.at[a, j]

    @pl.loop(0, NB)
    def _(i):
        q = qbuf[rows(i), :]
        low = lo[0:1, rows(i)] - i * T
        top = None
        for b in range(WIN):
            scores = nt(kbuf[rows(i + b), :], q)
            seen = r_i + b * T >= low
            if b == WIN - 1:
                seen = seen & (r_i <= t_i)
            scores = jnp.where(seen, scores, NEG)
            sbuf[b * T : (b + 1) * T, :] = scores
            part = fold(scores, jnp.maximum)
            top = part if top is None else jnp.maximum(top, part)
        top = jnp.max(top, axis=0, keepdims=True) * SCALE
        total = None
        att = None
        for b in range(WIN):
            p = jnp.exp2(sbuf[b * T : (b + 1) * T, :] * SCALE - top)
            part = fold(p, jnp.add)
            total = part if total is None else total + part
            pb = p.astype(BF)
            pbuf[rows(i * WIN + b), :] = pb
            term = nn(vT[:, rows(i + b)], pb)
            att = term if att is None else att + term
        inv = 1.0 / jnp.sum(total, axis=0, keepdims=True)
        linv[rows(i, 8), :] = jnp.broadcast_to(inv, (8, T))
        att = (att * inv).astype(BF)
        oT[rows(i, HD), :] = att
        oout[rows(i), :] = att.T
        send_peer(*out_args(0, i))

    for j in range(NB):
        arrived(*in_dst(3, j))

    def back(a, u):
        src, dst = ((hvo, hvi), (hko, hki))[a]
        return remote(src.at[rows(u)], dst.at[rows(u)], hg_send.at[a, u], hg_recv.at[a, u], h_prev)

    @pl.loop(0, NB)
    def _(i):
        q = qbuf[rows(i), :]
        inv = linv[rows(i, 8), :][0:1]
        doT = dobuf[rows(i), :].astype(F32).T * inv
        delta = jnp.sum(doT * oT[rows(i, HD), :].astype(F32), axis=0, keepdims=True)
        doT = doT.astype(BF)
        do = doT.T
        gq = None
        for b in range(WIN):
            pb = pbuf[rows(i * WIN + b), :]
            dvacc[rows(i + b), :] += nn(pb, do)
            dp = nn(vbuf[rows(i + b), :], doT)
            ds = (pb.astype(F32) * (dp - delta)).astype(BF)
            term = nn(kT[:, rows(i + b)], ds)
            gq = term if gq is None else gq + term
            dkacc[rows(i + b), :] += nn(ds, q)
        dqout[rows(i), :] = (gq * FACTOR).astype(BF).T
        send_peer(*out_args(1, i))
        hvo[rows(i), :] = dvacc[rows(i), :].astype(BF)
        back(0, i).start()
        hko[rows(i), :] = dkacc[rows(i), :].astype(BF)
        back(1, i).start()

    for j in range(NB):
        arrived(*out_dst(0, j))

    def o_rows(first_row):
        return jnp.concatenate(
            [oin[pl.ds(pl.multiple_of(j * T + first_row * ROWS, ROWS), ROWS), :] for j in range(NB)],
            axis=1,
        )

    other = jnp.concatenate([o_rows(1 - c), o_rows(3 - c)], axis=0)
    pa_out[...] = nn(other, wbuf[...]).astype(BF)
    pr_a = remote(pa_out, pa_in, pr_send.at[0], pr_recv.at[0], sib)
    pr_a.start()

    far = nn(o_rows(c + 2 * (1 - yl)), wbuf[...])
    arrived(pa_in, pr_recv.at[0])
    pb_out[...] = (far + pa_in[rows(1 - yl, ROWS), :].astype(F32)).astype(BF)
    pr_b = remote(pb_out, pb_in, pr_send.at[1], pr_recv.at[1], across)
    pr_b.start()
    near = nn(o_rows(h), wbuf[...]) + pa_in[rows(yl, ROWS), :].astype(F32)

    for u in range(NB):
        arrived(hvi.at[rows(u)], hg_recv.at[0, u])
        dvout[rows(u), :] = (dvacc[rows(NB + u), :] + hvi[rows(u), :].astype(F32)).astype(BF)
        send_peer(*out_args(2, u))
        arrived(hki.at[rows(u)], hg_recv.at[1, u])
        own = dkacc[rows(NB + u), :] + hki[rows(u), :].astype(F32)
        dkout[rows(u), :] = (own * FACTOR).astype(BF)
        send_peer(*out_args(3, u))

    arrived(pb_in, pr_recv.at[1])
    proj_ref[...] = (near + pb_in[...].astype(F32)).astype(BF)

    for a in range(1, 4):
        for j in range(NB):
            arrived(*out_dst(a, j))
            src = (dqin, dvin, dkin)[a - 1]
            (dq_ref, dv_ref, dk_ref)[a - 1][:, j, :] = src[j * T : (j + 1) * T, :]

    for a in range(4):
        for i in range(NB):
            sent_peer(*in_args(a, i))
            sent_peer(*out_args(a, i))
    for a in range(2):
        for j in range(NB):
            halo(a, j).wait_send()
            back(a, j).wait_send()
    for copy in (cot_x, cot_s, cot_f, pr_a, pr_b):
        copy.wait_send()


def drain(*refs):
    for n in range(4):
        refs[4+n][...]=refs[n][...]


def per_device(seq_size, queries, keys, values, out_weight, cotangent, doc_lengths):
    hbm = pl.BlockSpec(memory_space=pltpu.HBM)
    vmem = pl.BlockSpec(memory_space=pltpu.VMEM)

    def sc(*shape, dtype=BF):
        return pltpu.VMEM(shape, dtype)

    dma = pltpu.SemaphoreType.DMA
    half = NB * T
    results = pl.pallas_call(
        functools.partial(kernel, seq_size),
        out_shape=[jax.ShapeDtypeStruct((ROWS, D), BF)]
        + [jax.ShapeDtypeStruct((T, NB, HD), BF)] * 3,
        in_specs=[hbm] * 6,
        out_specs=[vmem] * 4,
        scratch_shapes=[
            sc(2 * half, HD),
            sc(2 * half, HD),
            sc(half, HD),
            sc(half, HD),
            sc(HD, 2 * half),
            sc(HD, 2 * half),
            sc(T, D),
            sc(NB * HD, D),
            sc(half, HD),
            sc(WIN * T, T, dtype=F32),
            sc(NB * WIN * T, T),
            sc(NB * HD, T),
            sc(NB * 8, T, dtype=F32),
            sc(8, half, dtype=jnp.int32),
            sc(2 * half, HD, dtype=F32),
            sc(2 * half, HD, dtype=F32),
            sc(half, HD),
            sc(half, HD),
            sc(half, HD),
            sc(half, HD),
            sc(half, HD),
            sc(half, HD),
            sc(half, HD),
            sc(half, HD),
            sc(T, NB, HD),
            sc(T, NB, HD),
            sc(T, NB, HD),
            sc(ROWS, D),
            sc(1, 128, dtype=jnp.int32),
            sc(half, HD),
            sc(half, HD),
            sc(half, HD),
            sc(half, HD),
            sc(half, HD),
            sc(half, HD),
            sc(half, HD),
            sc(2 * ROWS, D),
            sc(2 * ROWS, D),
            sc(ROWS, D),
            sc(ROWS, D),
            dma((4, NB)),
            dma((4, NB)),
            dma((2, NB)),
            dma((2, NB)),
            dma((3,)),
            dma((3,)),
            dma((4, NB)),
            dma((4, NB)),
            dma((2, NB)),
            dma((2, NB)),
            dma((2,)),
            dma((2,)),
            dma((6,)),
        ],
        compiler_params=pltpu.CompilerParams(
            collective_id=0, has_side_effects=True, vmem_limit_bytes=60 * 1024 * 1024
        ),
        name="ring_attention",
    )(queries, keys, values, out_weight, cotangent, doc_lengths.reshape(1, -1))
    return pl.pallas_call(
        drain,
        out_shape=[jax.ShapeDtypeStruct(x.shape, x.dtype) for x in results],
        in_specs=[vmem] * 4,
        out_specs=[vmem] * 4,
        name="drain",
    )(*results)


def solution(mesh):
    seq_head = P("seq", "head", None)
    rows = P(("seq", "head"), None)
    return jax.shard_map(
        functools.partial(per_device, mesh.shape["seq"]),
        mesh=mesh,
        in_specs=(seq_head, seq_head, seq_head, P("head", None), rows, P()),
        out_specs=(rows, seq_head, seq_head, seq_head),
        check_vma=False,
    )
```

```python
import functools
import math

import jax
import jax.numpy as jnp
from jax import lax
from jax.experimental import pallas as pl
from jax.experimental.pallas import tpu as pltpu
from jax.sharding import PartitionSpec as P

MESH = pl.DeviceIdType.MESH
T = 256
HD = 128
NB = 4
RING = 8
WIN = 5
D = 2048
ROWS = 64
NEG = -1e30
FACTOR = HD ** (-0.5)
SCALE = FACTOR * math.log2(math.e)
BF = jnp.bfloat16
F32 = jnp.float32


def nt(a, b):
    return lax.dot_general(a, b, (((1,), (1,)), ((), ())), preferred_element_type=F32)


def nn(a, b):
    return jnp.dot(a, b, preferred_element_type=F32)


def fold(x, op):
    parts = [x[r : r + 8] for r in range(0, x.shape[0], 8)]
    while len(parts) > 1:
        parts = [
            op(parts[j], parts[j + 1]) if j + 1 < len(parts) else parts[j]
            for j in range(0, len(parts), 2)
        ]
    return parts[0]


def kernel(
    seq_size,
    q_hbm,
    k_hbm,
    v_hbm,
    w_hbm,
    cot_hbm,
    len_hbm,
    proj_hbm,
    dq_hbm,
    dk_hbm,
    dv_hbm,
    kbuf,
    vbuf,
    qbuf,
    dobuf,
    kT,
    vT,
    cotbuf,
    wbuf,
    doloc,
    sbuf,
    pbuf,
    oT,
    linv,
    doT,
    deltas,
    lo,
    dkacc,
    dvacc,
    hko,
    hvo,
    hki,
    hvi,
    oout,
    dqout,
    dkout,
    dvout,
    proj_ref,
    dq_ref,
    dk_ref,
    dv_ref,
    k_ref,
    v_ref,
    q_ref,
    cot_ref,
    len_ref,
    kloc,
    vloc,
    qloc,
    oin,
    dqin,
    dvin,
    dkin,
    pa_out,
    pa_in,
    pb_out,
    pb_in,
    in_send,
    in_recv,
    halo_send,
    halo_recv,
    cot_send,
    cot_recv,
    out_send,
    out_recv,
    hg_send,
    hg_recv,
    pr_send,
    pr_recv,
    w_sem,
    r_sem,
):
    s = lax.axis_index("seq")
    h = lax.axis_index("head")
    z = lax.rem(s, RING)
    base = s - z
    c = lax.rem(h, 2)
    yl = h // 2
    half = z // NB
    zi = lax.rem(z, NB)
    sib = (s, h + 1 - 2 * c)
    across = (s, lax.rem(h + 2, 4))
    h_next = (lax.rem(s + RING * c, seq_size), h + 1 - 2 * c)
    h_prev = (lax.rem(s + seq_size - RING * (1 - c), seq_size), h + 1 - 2 * c)
    ring_adj = (lax.rem(s + seq_size + RING * (2 * c - 1), seq_size), h + 1 - 2 * c)

    no_halo_in = (s < RING) & (c == 0)
    no_halo_out = (s >= seq_size - RING) & (c == 1)
    alone = no_halo_in | no_halo_out

    def peer(i):
        return (base + NB * c + i, h - c + half)

    def is_self(i):
        return (c == half) & (zi == i)

    loads = [
        pltpu.make_async_copy(src, dst, w_sem.at[n])
        for n, (src, dst) in enumerate(
            (
                (k_hbm, k_ref),
                (v_hbm, v_ref),
                (q_hbm, q_ref),
                (cot_hbm, cot_ref),
                (len_hbm, len_ref),
                (w_hbm, wbuf),
            )
        )
    ]
    for copy in loads[:5]:
        copy.start()

    barrier = pltpu.get_barrier_semaphore()
    for dev in (sib, across):
        pl.semaphore_signal(barrier, inc=1, device_id=dev, device_id_type=MESH)

    @pl.when(jnp.logical_not(alone))
    def _():
        pl.semaphore_signal(barrier, inc=1, device_id=ring_adj, device_id_type=MESH)

    for i in range(NB):

        @pl.when(jnp.logical_not(is_self(i)))
        def _():
            pl.semaphore_signal(barrier, inc=1, device_id=peer(i), device_id_type=MESH)

    def remote(src, dst, ssem, rsem, dev):
        return pltpu.make_async_remote_copy(
            src_ref=src, dst_ref=dst, send_sem=ssem, recv_sem=rsem, device_id=dev, device_id_type=MESH
        )

    def rows(i, n=T):
        return pl.ds(pl.multiple_of(i * n, n), n)

    def send_peer(i, src, dst, ssem, rsem):
        @pl.when(jnp.logical_not(is_self(i)))
        def _():
            remote(src, dst, ssem, rsem, peer(i)).start()

        @pl.when(is_self(i))
        def _():
            pltpu.make_async_copy(src, dst, rsem).start()

    def sent_peer(i, src, dst, ssem, rsem):
        @pl.when(jnp.logical_not(is_self(i)))
        def _():
            remote(src, dst, ssem, rsem, peer(i)).wait_send()

    def arrived(dst, rsem):
        pltpu.make_async_copy(dst, dst, rsem).wait()

    def split(src, dst, i):
        dst[i * T : (i + 1) * T, :] = src[:, i, :]


    def in_args(a, i):
        src = (kloc, vloc, qloc, doloc)[a].at[rows(i)]
        if a < 2:
            dst = (kbuf, vbuf)[a].at[rows(NB + zi)]
        else:
            dst = (qbuf, dobuf)[a - 2].at[rows(zi)]
        return i, src, dst, in_send.at[a, i], in_recv.at[a, zi]

    def in_dst(a, j):
        if a < 2:
            return (kbuf, vbuf)[a].at[rows(NB + j)], in_recv.at[a, j]
        return (qbuf, dobuf)[a - 2].at[rows(j)], in_recv.at[a, j]

    loads[0].wait()
    loads[5].start()
    for i in range(NB):
        split(k_ref, kloc, i)
    loads[3].wait()
    pl.semaphore_wait(barrier, 5 + jnp.where(c != half, 1, 0) + jnp.where(alone, 0, 1))

    for i in range(NB):
        send_peer(*in_args(0, i))
    def cot_rows(g):
        return cotbuf.at[rows(g, ROWS)]

    cot_x = remote(cot_ref, cot_rows(h), cot_send.at[0], cot_recv.at[0], across)
    cot_s = remote(cot_ref, cot_rows(h), cot_send.at[1], cot_recv.at[1], sib)
    cot_x.start()
    cot_s.start()
    for a in (1, 2):
        loads[a].wait()
        for i in range(NB):
            split((k_ref, v_ref, q_ref)[a], (kloc, vloc, qloc)[a], i)
    cotbuf[rows(h, ROWS), :] = cot_ref[...]

    loads[4].wait()
    lens = len_ref[...].astype(F32)
    d_i = lax.broadcasted_iota(jnp.int32, (128, 128), 0)
    e_i = lax.broadcasted_iota(jnp.int32, (128, 128), 1)
    starts = jnp.sum(jnp.where(e_i < d_i, jnp.broadcast_to(lens, (128, 128)), 0.0), axis=1, keepdims=True)
    first = (base + NB * c) * T
    pos = (first + lax.broadcasted_iota(jnp.int32, (128, NB * T), 1)).astype(F32)
    started = jnp.where(jnp.broadcast_to(starts, (128, NB * T)) <= pos, starts, 0.0)
    low = jnp.max(started, axis=0, keepdims=True).astype(jnp.int32) - (first - NB * T)
    lo[...] = jnp.broadcast_to(low, (8, NB * T))
    @pl.when(no_halo_in)
    def _():
        for buf in (kbuf, vbuf):
            buf[0 : NB * T, :] = jnp.zeros((NB * T, HD), BF)

    @pl.when(no_halo_out)
    def _():
        for buf in (hki, hvi):
            buf[...] = jnp.zeros_like(buf)

    dkacc[...] = jnp.zeros_like(dkacc)
    dvacc[...] = jnp.zeros_like(dvacc)

    def halo(a, j):
        buf = (kbuf, vbuf)[a]
        return remote(buf.at[rows(NB + j)], buf.at[rows(j)], halo_send.at[a, j], halo_recv.at[a, j], h_next)

    cot_f = remote(
        cot_rows(across[1]), cot_rows(across[1]), cot_send.at[2], cot_recv.at[2], sib
    )
    for i in range(NB):
        sent_peer(*in_args(0, i))
    for i in range(NB):
        send_peer(*in_args(1, i))
    for i in range(NB):
        send_peer(*in_args(2, i))
    for j in range(NB):
        arrived(*in_dst(0, j))
        pl.when(jnp.logical_not(no_halo_out))(halo(0, j).start)
    arrived(cot_rows(across[1]), cot_recv.at[0])
    cot_f.start()

    loads[5].wait()
    arrived(cot_rows(sib[1]), cot_recv.at[1])
    arrived(cot_rows(lax.rem(sib[1] + 2, 4)), cot_recv.at[2])
    d_att = nt(cotbuf[...], wbuf[...]).astype(BF)
    for i in range(NB):
        doloc[i * T : (i + 1) * T, :] = d_att[:, i * HD : (i + 1) * HD]
        send_peer(*in_args(3, i))

    for j in range(NB):
        arrived(*in_dst(1, j))
        pl.when(jnp.logical_not(no_halo_out))(halo(1, j).start)

    @pl.when(jnp.logical_not(no_halo_in))
    def _():
        for a in range(2):
            for j in range(NB):
                arrived((kbuf, vbuf)[a].at[rows(j)], halo_recv.at[a, j])

    for b in range(2 * NB):
        kT[:, b * T : (b + 1) * T] = kbuf[b * T : (b + 1) * T, :].T
        vT[:, b * T : (b + 1) * T] = vbuf[b * T : (b + 1) * T, :].T
    for j in range(NB):
        arrived(*in_dst(2, j))

    r_i = lax.broadcasted_iota(jnp.int32, (T, T), 0)
    t_i = lax.broadcasted_iota(jnp.int32, (T, T), 1)

    def out_args(a, i):
        src = (oout, dqout, dvout, dkout)[a].at[rows(i)]
        dst = (oin, dqin, dvin, dkin)[a].at[rows(zi)]
        return i, src, dst, out_send.at[a, i], out_recv.at[a, zi]

    def out_dst(a, j):
        return (oin, dqin, dvin, dkin)[a].at[rows(j)], out_recv.at[a, j]

    @pl.loop(0, NB)
    def _(i):
        q = qbuf[rows(i), :]
        low = lo[0:1, rows(i)] - i * T
        top = None
        for b in range(WIN):
            scores = nt(kbuf[rows(i + b), :], q)
            seen = r_i + b * T >= low
            if b == WIN - 1:
                seen = seen & (r_i <= t_i)
            scores = jnp.where(seen, scores, NEG)
            sbuf[b * T : (b + 1) * T, :] = scores
            part = fold(scores, jnp.maximum)
            top = part if top is None else jnp.maximum(top, part)
        top = jnp.max(top, axis=0, keepdims=True) * SCALE
        total = None
        att = None
        for b in range(WIN):
            p = jnp.exp2(sbuf[b * T : (b + 1) * T, :] * SCALE - top)
            part = fold(p, jnp.add)
            total = part if total is None else total + part
            pb = p.astype(BF)
            pbuf[rows(i * WIN + b), :] = pb
            term = nn(vT[:, rows(i + b)], pb)
            att = term if att is None else att + term
        inv = 1.0 / jnp.sum(total, axis=0, keepdims=True)
        linv[rows(i, 8), :] = jnp.broadcast_to(inv, (8, T))
        att = (att * inv).astype(BF)
        oT[rows(i, HD), :] = att
        oout[rows(i), :] = att.T
        send_peer(*out_args(0, i))

    for j in range(NB):
        arrived(*in_dst(3, j))

    def back(a, u):
        src, dst = ((hvo, hvi), (hko, hki))[a]
        return remote(src.at[rows(u)], dst.at[rows(u)], hg_send.at[a, u], hg_recv.at[a, u], h_prev)

    @pl.loop(0, NB)
    def _(i):
        inv = linv[rows(i, 8), :][0:1]
        scaled = dobuf[rows(i), :].astype(F32).T * inv
        delta = jnp.sum(scaled * oT[rows(i, HD), :].astype(F32), axis=0, keepdims=True)
        deltas[rows(i, 8), :] = jnp.broadcast_to(delta, (8, T))
        scaled = scaled.astype(BF)
        doT[rows(i, HD), :] = scaled
        do = scaled.T
        for b in range(WIN):
            dvacc[rows(i + b), :] += nn(pbuf[rows(i * WIN + b), :], do)
        hvo[rows(i), :] = dvacc[rows(i), :].astype(BF)
        pl.when(jnp.logical_not(no_halo_in))(back(0, i).start)

    @pl.loop(0, NB)
    def _(i):
        q = qbuf[rows(i), :]
        delta = deltas[rows(i, 8), :][0:1]
        scaled = doT[rows(i, HD), :]
        gq = None
        for b in range(WIN):
            pb = pbuf[rows(i * WIN + b), :]
            dp = nn(vbuf[rows(i + b), :], scaled)
            ds = (pb.astype(F32) * (dp - delta)).astype(BF)
            term = nn(kT[:, rows(i + b)], ds)
            gq = term if gq is None else gq + term
            dkacc[rows(i + b), :] += nn(ds, q)
        hko[rows(i), :] = dkacc[rows(i), :].astype(BF)
        pl.when(jnp.logical_not(no_halo_in))(back(1, i).start)
        dqout[rows(i), :] = (gq * FACTOR).astype(BF).T
        send_peer(*out_args(1, i))

    for j in range(NB):
        arrived(*out_dst(0, j))

    def o_rows(first_row):
        return jnp.concatenate(
            [oin[pl.ds(pl.multiple_of(j * T + first_row * ROWS, ROWS), ROWS), :] for j in range(NB)],
            axis=1,
        )

    other = jnp.concatenate([o_rows(1 - c), o_rows(3 - c)], axis=0)
    pa_out[...] = nn(other, wbuf[...]).astype(BF)
    pr_a = remote(pa_out, pa_in, pr_send.at[0], pr_recv.at[0], sib)
    pr_a.start()

    far = nn(o_rows(c + 2 * (1 - yl)), wbuf[...])
    arrived(pa_in, pr_recv.at[0])
    pb_out[...] = (far + pa_in[rows(1 - yl, ROWS), :].astype(F32)).astype(BF)
    pr_b = remote(pb_out, pb_in, pr_send.at[1], pr_recv.at[1], across)
    pr_b.start()
    near = nn(o_rows(h), wbuf[...]) + pa_in[rows(yl, ROWS), :].astype(F32)

    for u in range(NB):

        @pl.when(jnp.logical_not(no_halo_out))
        def _():
            arrived(hvi.at[rows(u)], hg_recv.at[0, u])

        dvout[rows(u), :] = (dvacc[rows(NB + u), :] + hvi[rows(u), :].astype(F32)).astype(BF)
        send_peer(*out_args(2, u))

        @pl.when(jnp.logical_not(no_halo_out))
        def _():
            arrived(hki.at[rows(u)], hg_recv.at[1, u])

        own = dkacc[rows(NB + u), :] + hki[rows(u), :].astype(F32)
        dkout[rows(u), :] = (own * FACTOR).astype(BF)
        send_peer(*out_args(3, u))

    arrived(pb_in, pr_recv.at[1])
    stores = [
        pltpu.make_async_copy(src, dst, r_sem.at[n])
        for n, (src, dst) in enumerate(
            ((dq_ref, dq_hbm), (dv_ref, dv_hbm), (dk_ref, dk_hbm), (proj_ref, proj_hbm))
        )
    ]
    proj_ref[...] = (near + pb_in[...].astype(F32)).astype(BF)
    stores[3].start()

    for a in range(1, 4):
        for j in range(NB):
            arrived(*out_dst(a, j))
            src = (dqin, dvin, dkin)[a - 1]
            (dq_ref, dv_ref, dk_ref)[a - 1][:, j, :] = src[j * T : (j + 1) * T, :]
        stores[a - 1].start()

    for a in range(4):
        for i in range(NB):
            if a > 0:
                sent_peer(*in_args(a, i))
            sent_peer(*out_args(a, i))
    for a in range(2):
        for j in range(NB):
            pl.when(jnp.logical_not(no_halo_out))(halo(a, j).wait_send)
            pl.when(jnp.logical_not(no_halo_in))(back(a, j).wait_send)
    for copy in stores:
        copy.wait()
    for copy in (cot_x, cot_s, cot_f, pr_a, pr_b):
        copy.wait_send()


def drain(*refs):
    src, dst, bufs = refs[:4], refs[4:8], refs[8:12]
    r_sem, w_sem = refs[12:]
    reads = [pltpu.make_async_copy(src[n], bufs[n], r_sem.at[n]) for n in range(4)]
    writes = [pltpu.make_async_copy(bufs[n], dst[n], w_sem.at[n]) for n in range(4)]
    for copy in reads:
        copy.start()
    for n in range(4):
        reads[n].wait()
        writes[n].start()
    for copy in writes:
        copy.wait()


def per_device(seq_size, queries, keys, values, out_weight, cotangent, doc_lengths):
    hbm = pl.BlockSpec(memory_space=pltpu.HBM)

    def sc(*shape, dtype=BF):
        return pltpu.VMEM(shape, dtype)

    dma = pltpu.SemaphoreType.DMA
    half = NB * T
    results = pl.pallas_call(
        functools.partial(kernel, seq_size),
        out_shape=[jax.ShapeDtypeStruct((ROWS, D), BF)]
        + [jax.ShapeDtypeStruct((T, NB, HD), BF)] * 3,
        in_specs=[hbm] * 6,
        out_specs=[hbm] * 4,
        scratch_shapes=[
            sc(2 * half, HD),
            sc(2 * half, HD),
            sc(half, HD),
            sc(half, HD),
            sc(HD, 2 * half),
            sc(HD, 2 * half),
            sc(T, D),
            sc(NB * HD, D),
            sc(half, HD),
            sc(WIN * T, T, dtype=F32),
            sc(NB * WIN * T, T),
            sc(NB * HD, T),
            sc(NB * 8, T, dtype=F32),
            sc(NB * HD, T),
            sc(NB * 8, T, dtype=F32),
            sc(8, half, dtype=jnp.int32),
            sc(2 * half, HD, dtype=F32),
            sc(2 * half, HD, dtype=F32),
            sc(half, HD),
            sc(half, HD),
            sc(half, HD),
            sc(half, HD),
            sc(half, HD),
            sc(half, HD),
            sc(half, HD),
            sc(half, HD),
            sc(ROWS, D),
            sc(T, NB, HD),
            sc(T, NB, HD),
            sc(T, NB, HD),
            sc(T, NB, HD),
            sc(T, NB, HD),
            sc(T, NB, HD),
            sc(ROWS, D),
            sc(1, 128, dtype=jnp.int32),
            sc(half, HD),
            sc(half, HD),
            sc(half, HD),
            sc(half, HD),
            sc(half, HD),
            sc(half, HD),
            sc(half, HD),
            sc(2 * ROWS, D),
            sc(2 * ROWS, D),
            sc(ROWS, D),
            sc(ROWS, D),
            dma((4, NB)),
            dma((4, NB)),
            dma((2, NB)),
            dma((2, NB)),
            dma((3,)),
            dma((3,)),
            dma((4, NB)),
            dma((4, NB)),
            dma((2, NB)),
            dma((2, NB)),
            dma((2,)),
            dma((2,)),
            dma((6,)),
            dma((4,)),
        ],
        compiler_params=pltpu.CompilerParams(
            collective_id=0, has_side_effects=True, vmem_limit_bytes=60 * 1024 * 1024
        ),
        name="ring_attention",
    )(queries, keys, values, out_weight, cotangent, doc_lengths.reshape(1, -1))
    return pl.pallas_call(
        drain,
        out_shape=[jax.ShapeDtypeStruct(x.shape, x.dtype) for x in results],
        in_specs=[pl.BlockSpec(memory_space=pl.ANY)] * 4,
        out_specs=[hbm] * 4,
        scratch_shapes=[sc(*x.shape) for x in results] + [dma((4,)), dma((4,))],
        compiler_params=pltpu.CompilerParams(vmem_limit_bytes=60 * 1024 * 1024),
        name="drain",
    )(*results)


def solution(mesh):
    seq_head = P("seq", "head", None)
    rows = P(("seq", "head"), None)
    return jax.shard_map(
        functools.partial(per_device, mesh.shape["seq"]),
        mesh=mesh,
        in_specs=(seq_head, seq_head, seq_head, P("head", None), rows, P()),
        out_specs=(rows, seq_head, seq_head, seq_head),
        check_vma=False,
    )
```

```python
import functools
import math

import jax
import jax.numpy as jnp
from jax import lax
from jax.experimental import pallas as pl
from jax.experimental.pallas import tpu as pltpu
from jax.sharding import PartitionSpec as P

MESH = pl.DeviceIdType.MESH
T = 256
HD = 128
NB = 4
RING = 8
WIN = 5
D = 2048
ROWS = 64
NEG = -1e30
FACTOR = HD ** (-0.5)
SCALE = FACTOR * math.log2(math.e)
BF = jnp.bfloat16
F32 = jnp.float32


def nt(a, b):
    return lax.dot_general(a, b, (((1,), (1,)), ((), ())), preferred_element_type=F32)


def nn(a, b):
    return jnp.dot(a, b, preferred_element_type=F32)


def fold(x, op):
    parts = [x[r : r + 8] for r in range(0, x.shape[0], 8)]
    while len(parts) > 1:
        parts = [
            op(parts[j], parts[j + 1]) if j + 1 < len(parts) else parts[j]
            for j in range(0, len(parts), 2)
        ]
    return parts[0]


def kernel(
    seq_size,
    q_hbm,
    k_hbm,
    v_hbm,
    w_hbm,
    cot_hbm,
    len_hbm,
    proj_hbm,
    dq_hbm,
    dk_hbm,
    dv_hbm,
    kbuf,
    vbuf,
    qbuf,
    dobuf,
    kT,
    vT,
    cotbuf,
    wbuf,
    doloc,
    sbuf,
    pbuf,
    oT,
    linv,
    doT,
    deltas,
    lo,
    dkacc,
    dvacc,
    hko,
    hvo,
    hki,
    hvi,
    oout,
    dqout,
    dkout,
    dvout,
    proj_ref,
    dq_ref,
    dk_ref,
    dv_ref,
    k_ref,
    v_ref,
    q_ref,
    cot_ref,
    len_ref,
    kloc,
    vloc,
    qloc,
    oin,
    dqin,
    dvin,
    dkin,
    pa_out,
    pa_in,
    pb_out,
    pb_in,
    in_send,
    in_recv,
    halo_send,
    halo_recv,
    cot_send,
    cot_recv,
    out_send,
    out_recv,
    hg_send,
    hg_recv,
    pr_send,
    pr_recv,
    w_sem,
    r_sem,
):
    s = lax.axis_index("seq")
    h = lax.axis_index("head")
    z = lax.rem(s, RING)
    base = s - z
    c = lax.rem(h, 2)
    yl = h // 2
    half = z // NB
    zi = lax.rem(z, NB)
    sib = (s, h + 1 - 2 * c)
    across = (s, lax.rem(h + 2, 4))
    h_next = (lax.rem(s + RING * c, seq_size), h + 1 - 2 * c)
    h_prev = (lax.rem(s + seq_size - RING * (1 - c), seq_size), h + 1 - 2 * c)
    ring_adj = (lax.rem(s + seq_size + RING * (2 * c - 1), seq_size), h + 1 - 2 * c)

    no_halo_in = (s < RING) & (c == 0)
    no_halo_out = (s >= seq_size - RING) & (c == 1)
    alone = no_halo_in | no_halo_out

    def peer(i):
        return (base + NB * c + i, h - c + half)

    def is_self(i):
        return (c == half) & (zi == i)

    loads = [
        pltpu.make_async_copy(src, dst, w_sem.at[n])
        for n, (src, dst) in enumerate(
            (
                (k_hbm, k_ref),
                (v_hbm, v_ref),
                (q_hbm, q_ref),
                (cot_hbm, cot_ref),
                (len_hbm, len_ref),
                (w_hbm, wbuf),
            )
        )
    ]
    for copy in loads[:5]:
        copy.start()

    barrier = pltpu.get_barrier_semaphore()
    for dev in (sib, across):
        pl.semaphore_signal(barrier, inc=1, device_id=dev, device_id_type=MESH)

    @pl.when(jnp.logical_not(alone))
    def _():
        pl.semaphore_signal(barrier, inc=1, device_id=ring_adj, device_id_type=MESH)

    for i in range(NB):

        @pl.when(jnp.logical_not(is_self(i)))
        def _():
            pl.semaphore_signal(barrier, inc=1, device_id=peer(i), device_id_type=MESH)

    def remote(src, dst, ssem, rsem, dev):
        return pltpu.make_async_remote_copy(
            src_ref=src, dst_ref=dst, send_sem=ssem, recv_sem=rsem, device_id=dev, device_id_type=MESH
        )

    def rows(i, n=T):
        return pl.ds(pl.multiple_of(i * n, n), n)

    def send_peer(i, src, dst, ssem, rsem):
        @pl.when(jnp.logical_not(is_self(i)))
        def _():
            remote(src, dst, ssem, rsem, peer(i)).start()

        @pl.when(is_self(i))
        def _():
            pltpu.make_async_copy(src, dst, rsem).start()

    def sent_peer(i, src, dst, ssem, rsem):
        @pl.when(jnp.logical_not(is_self(i)))
        def _():
            remote(src, dst, ssem, rsem, peer(i)).wait_send()

    def arrived(dst, rsem):
        pltpu.make_async_copy(dst, dst, rsem).wait()

    def split(src, dst, i):
        dst[i * T : (i + 1) * T, :] = src[:, i, :]


    def in_args(a, i):
        src = (kloc, vloc, qloc, doloc)[a].at[rows(i)]
        if a < 2:
            dst = (kbuf, vbuf)[a].at[rows(NB + zi)]
        else:
            dst = (qbuf, dobuf)[a - 2].at[rows(zi)]
        return i, src, dst, in_send.at[a, i], in_recv.at[a, zi]

    def in_dst(a, j):
        if a < 2:
            return (kbuf, vbuf)[a].at[rows(NB + j)], in_recv.at[a, j]
        return (qbuf, dobuf)[a - 2].at[rows(j)], in_recv.at[a, j]

    loads[0].wait()
    loads[5].start()
    for i in range(NB):
        split(k_ref, kloc, i)
    loads[3].wait()
    pl.semaphore_wait(barrier, 5 + jnp.where(c != half, 1, 0) + jnp.where(alone, 0, 1))

    for i in range(NB):
        send_peer(*in_args(0, i))
    def cot_rows(g):
        return cotbuf.at[rows(g, ROWS)]

    cot_x = remote(cot_ref, cot_rows(h), cot_send.at[0], cot_recv.at[0], across)
    cot_s = remote(cot_ref, cot_rows(h), cot_send.at[1], cot_recv.at[1], sib)
    cot_x.start()
    cot_s.start()
    for a in (1, 2):
        loads[a].wait()
        for i in range(NB):
            split((k_ref, v_ref, q_ref)[a], (kloc, vloc, qloc)[a], i)
    cotbuf[rows(h, ROWS), :] = cot_ref[...]

    loads[4].wait()
    lens = len_ref[...].astype(F32)
    d_i = lax.broadcasted_iota(jnp.int32, (128, 128), 0)
    e_i = lax.broadcasted_iota(jnp.int32, (128, 128), 1)
    starts = jnp.sum(jnp.where(e_i < d_i, jnp.broadcast_to(lens, (128, 128)), 0.0), axis=1, keepdims=True)
    first = (base + NB * c) * T
    pos = (first + lax.broadcasted_iota(jnp.int32, (128, NB * T), 1)).astype(F32)
    started = jnp.where(jnp.broadcast_to(starts, (128, NB * T)) <= pos, starts, 0.0)
    low = jnp.max(started, axis=0, keepdims=True).astype(jnp.int32) - (first - NB * T)
    lo[...] = jnp.broadcast_to(low, (8, NB * T))
    @pl.when(no_halo_in)
    def _():
        for buf in (kbuf, vbuf):
            buf[0 : NB * T, :] = jnp.zeros((NB * T, HD), BF)

    @pl.when(no_halo_out)
    def _():
        for buf in (hki, hvi):
            buf[...] = jnp.zeros_like(buf)

    dkacc[...] = jnp.zeros_like(dkacc)
    dvacc[...] = jnp.zeros_like(dvacc)

    def halo(a, j):
        buf = (kbuf, vbuf)[a]
        return remote(buf.at[rows(NB + j)], buf.at[rows(j)], halo_send.at[a, j], halo_recv.at[a, j], h_next)

    cot_f = remote(
        cot_rows(across[1]), cot_rows(across[1]), cot_send.at[2], cot_recv.at[2], sib
    )
    for i in range(NB):
        sent_peer(*in_args(0, i))
    for i in range(NB):
        send_peer(*in_args(1, i))
    for i in range(NB):
        send_peer(*in_args(2, i))
    for j in range(NB):
        arrived(*in_dst(0, j))
        pl.when(jnp.logical_not(no_halo_out))(halo(0, j).start)
    arrived(cot_rows(across[1]), cot_recv.at[0])
    cot_f.start()

    loads[5].wait()
    arrived(cot_rows(sib[1]), cot_recv.at[1])
    arrived(cot_rows(lax.rem(sib[1] + 2, 4)), cot_recv.at[2])
    d_att = nt(cotbuf[...], wbuf[...]).astype(BF)
    for i in range(NB):
        doloc[i * T : (i + 1) * T, :] = d_att[:, i * HD : (i + 1) * HD]
        send_peer(*in_args(3, i))

    for j in range(NB):
        arrived(*in_dst(1, j))
        pl.when(jnp.logical_not(no_halo_out))(halo(1, j).start)

    @pl.when(jnp.logical_not(no_halo_in))
    def _():
        for a in range(2):
            for j in range(NB):
                arrived((kbuf, vbuf)[a].at[rows(j)], halo_recv.at[a, j])

    for b in range(2 * NB):
        kT[:, b * T : (b + 1) * T] = kbuf[b * T : (b + 1) * T, :].T
        vT[:, b * T : (b + 1) * T] = vbuf[b * T : (b + 1) * T, :].T
    for j in range(NB):
        arrived(*in_dst(2, j))

    r_i = lax.broadcasted_iota(jnp.int32, (T, T), 0)
    t_i = lax.broadcasted_iota(jnp.int32, (T, T), 1)

    def out_args(a, i):
        src = (oout, dqout, dvout, dkout)[a].at[rows(i)]
        dst = (oin, dqin, dvin, dkin)[a].at[rows(zi)]
        return i, src, dst, out_send.at[a, i], out_recv.at[a, zi]

    def out_dst(a, j):
        return (oin, dqin, dvin, dkin)[a].at[rows(j)], out_recv.at[a, j]

    @pl.loop(0, NB)
    def _(i):
        q = qbuf[rows(i), :]
        low = lo[0:1, rows(i)] - i * T
        top = None
        for b in range(WIN):
            scores = nt(kbuf[rows(i + b), :], q)
            seen = r_i + b * T >= low
            if b == WIN - 1:
                seen = seen & (r_i <= t_i)
            scores = jnp.where(seen, scores, NEG)
            sbuf[b * T : (b + 1) * T, :] = scores
            part = fold(scores, jnp.maximum)
            top = part if top is None else jnp.maximum(top, part)
        top = jnp.max(top, axis=0, keepdims=True) * SCALE
        total = None
        att = None
        for b in range(WIN):
            p = jnp.exp2(sbuf[b * T : (b + 1) * T, :] * SCALE - top)
            part = fold(p, jnp.add)
            total = part if total is None else total + part
            pb = p.astype(BF)
            pbuf[rows(i * WIN + b), :] = pb
            term = nn(vT[:, rows(i + b)], pb)
            att = term if att is None else att + term
        inv = 1.0 / jnp.sum(total, axis=0, keepdims=True)
        linv[rows(i, 8), :] = jnp.broadcast_to(inv, (8, T))
        att = (att * inv).astype(BF)
        oT[rows(i, HD), :] = att
        oout[rows(i), :] = att.T
        send_peer(*out_args(0, i))

    for j in range(NB):
        arrived(*in_dst(3, j))

    def back(a, u):
        src, dst = ((hvo, hvi), (hko, hki))[a]
        return remote(src.at[rows(u)], dst.at[rows(u)], hg_send.at[a, u], hg_recv.at[a, u], h_prev)

    @pl.loop(0, NB)
    def _(i):
        inv = linv[rows(i, 8), :][0:1]
        scaled = dobuf[rows(i), :].astype(F32).T * inv
        delta = jnp.sum(scaled * oT[rows(i, HD), :].astype(F32), axis=0, keepdims=True)
        deltas[rows(i, 8), :] = jnp.broadcast_to(delta, (8, T))
        scaled = scaled.astype(BF)
        doT[rows(i, HD), :] = scaled
        do = scaled.T
        for b in range(WIN):
            dvacc[rows(i + b), :] += nn(pbuf[rows(i * WIN + b), :], do)
        hvo[rows(i), :] = dvacc[rows(i), :].astype(BF)
        pl.when(jnp.logical_not(no_halo_in))(back(0, i).start)

    @pl.loop(0, NB)
    def _(i):
        q = qbuf[rows(i), :]
        delta = deltas[rows(i, 8), :][0:1]
        scaled = doT[rows(i, HD), :]
        gq = None
        for b in range(WIN):
            pb = pbuf[rows(i * WIN + b), :]
            dp = nn(vbuf[rows(i + b), :], scaled)
            ds = (pb.astype(F32) * (dp - delta)).astype(BF)
            term = nn(kT[:, rows(i + b)], ds)
            gq = term if gq is None else gq + term
            dkacc[rows(i + b), :] += nn(ds, q)
        hko[rows(i), :] = dkacc[rows(i), :].astype(BF)
        pl.when(jnp.logical_not(no_halo_in))(back(1, i).start)
        dqout[rows(i), :] = (gq * FACTOR).astype(BF).T
        send_peer(*out_args(1, i))

    def return_keys():
        for u in range(NB):

            @pl.when(jnp.logical_not(no_halo_out))
            def _():
                arrived(hvi.at[rows(u)], hg_recv.at[0, u])

            dvout[rows(u), :] = (dvacc[rows(NB + u), :] + hvi[rows(u), :].astype(F32)).astype(BF)
            send_peer(*out_args(2, u))

            @pl.when(jnp.logical_not(no_halo_out))
            def _():
                arrived(hki.at[rows(u)], hg_recv.at[1, u])

            own = dkacc[rows(NB + u), :] + hki[rows(u), :].astype(F32)
            dkout[rows(u), :] = (own * FACTOR).astype(BF)
            send_peer(*out_args(3, u))

    pl.when(c == 0)(return_keys)

    for j in range(NB):
        arrived(*out_dst(0, j))

    def o_rows(first_row):
        return jnp.concatenate(
            [oin[pl.ds(pl.multiple_of(j * T + first_row * ROWS, ROWS), ROWS), :] for j in range(NB)],
            axis=1,
        )

    other = jnp.concatenate([o_rows(1 - c), o_rows(3 - c)], axis=0)
    pa_out[...] = nn(other, wbuf[...]).astype(BF)
    pr_a = remote(pa_out, pa_in, pr_send.at[0], pr_recv.at[0], sib)
    pr_a.start()

    far = nn(o_rows(c + 2 * (1 - yl)), wbuf[...])
    arrived(pa_in, pr_recv.at[0])
    pb_out[...] = (far + pa_in[rows(1 - yl, ROWS), :].astype(F32)).astype(BF)
    pr_b = remote(pb_out, pb_in, pr_send.at[1], pr_recv.at[1], across)
    pr_b.start()
    near = nn(o_rows(h), wbuf[...]) + pa_in[rows(yl, ROWS), :].astype(F32)

    pl.when(c == 1)(return_keys)

    arrived(pb_in, pr_recv.at[1])
    stores = [
        pltpu.make_async_copy(src, dst, r_sem.at[n])
        for n, (src, dst) in enumerate(
            ((dq_ref, dq_hbm), (dv_ref, dv_hbm), (dk_ref, dk_hbm), (proj_ref, proj_hbm))
        )
    ]
    proj_ref[...] = (near + pb_in[...].astype(F32)).astype(BF)
    stores[3].start()

    for a in range(1, 4):
        for j in range(NB):
            arrived(*out_dst(a, j))
            src = (dqin, dvin, dkin)[a - 1]
            (dq_ref, dv_ref, dk_ref)[a - 1][:, j, :] = src[j * T : (j + 1) * T, :]
        stores[a - 1].start()

    for a in range(4):
        for i in range(NB):
            if a > 0:
                sent_peer(*in_args(a, i))
            sent_peer(*out_args(a, i))
    for a in range(2):
        for j in range(NB):
            pl.when(jnp.logical_not(no_halo_out))(halo(a, j).wait_send)
            pl.when(jnp.logical_not(no_halo_in))(back(a, j).wait_send)
    for copy in stores:
        copy.wait()
    for copy in (cot_x, cot_s, cot_f, pr_a, pr_b):
        copy.wait_send()


def drain(*refs):
    src, dst, bufs = refs[:4], refs[4:8], refs[8:12]
    r_sem, w_sem = refs[12:]
    reads = [pltpu.make_async_copy(src[n], bufs[n], r_sem.at[n]) for n in range(4)]
    writes = [pltpu.make_async_copy(bufs[n], dst[n], w_sem.at[n]) for n in range(4)]
    for copy in reads:
        copy.start()
    for n in range(4):
        reads[n].wait()
        writes[n].start()
    for copy in writes:
        copy.wait()


def per_device(seq_size, queries, keys, values, out_weight, cotangent, doc_lengths):
    hbm = pl.BlockSpec(memory_space=pltpu.HBM)

    def sc(*shape, dtype=BF):
        return pltpu.VMEM(shape, dtype)

    dma = pltpu.SemaphoreType.DMA
    half = NB * T
    results = pl.pallas_call(
        functools.partial(kernel, seq_size),
        out_shape=[jax.ShapeDtypeStruct((ROWS, D), BF)]
        + [jax.ShapeDtypeStruct((T, NB, HD), BF)] * 3,
        in_specs=[hbm] * 6,
        out_specs=[hbm] * 4,
        scratch_shapes=[
            sc(2 * half, HD),
            sc(2 * half, HD),
            sc(half, HD),
            sc(half, HD),
            sc(HD, 2 * half),
            sc(HD, 2 * half),
            sc(T, D),
            sc(NB * HD, D),
            sc(half, HD),
            sc(WIN * T, T, dtype=F32),
            sc(NB * WIN * T, T),
            sc(NB * HD, T),
            sc(NB * 8, T, dtype=F32),
            sc(NB * HD, T),
            sc(NB * 8, T, dtype=F32),
            sc(8, half, dtype=jnp.int32),
            sc(2 * half, HD, dtype=F32),
            sc(2 * half, HD, dtype=F32),
            sc(half, HD),
            sc(half, HD),
            sc(half, HD),
            sc(half, HD),
            sc(half, HD),
            sc(half, HD),
            sc(half, HD),
            sc(half, HD),
            sc(ROWS, D),
            sc(T, NB, HD),
            sc(T, NB, HD),
            sc(T, NB, HD),
            sc(T, NB, HD),
            sc(T, NB, HD),
            sc(T, NB, HD),
            sc(ROWS, D),
            sc(1, 128, dtype=jnp.int32),
            sc(half, HD),
            sc(half, HD),
            sc(half, HD),
            sc(half, HD),
            sc(half, HD),
            sc(half, HD),
            sc(half, HD),
            sc(2 * ROWS, D),
            sc(2 * ROWS, D),
            sc(ROWS, D),
            sc(ROWS, D),
            dma((4, NB)),
            dma((4, NB)),
            dma((2, NB)),
            dma((2, NB)),
            dma((3,)),
            dma((3,)),
            dma((4, NB)),
            dma((4, NB)),
            dma((2, NB)),
            dma((2, NB)),
            dma((2,)),
            dma((2,)),
            dma((6,)),
            dma((4,)),
        ],
        compiler_params=pltpu.CompilerParams(
            collective_id=0, has_side_effects=True, vmem_limit_bytes=60 * 1024 * 1024
        ),
        name="ring_attention",
    )(queries, keys, values, out_weight, cotangent, doc_lengths.reshape(1, -1))
    return pl.pallas_call(
        drain,
        out_shape=[jax.ShapeDtypeStruct(x.shape, x.dtype) for x in results],
        in_specs=[pl.BlockSpec(memory_space=pl.ANY)] * 4,
        out_specs=[hbm] * 4,
        scratch_shapes=[sc(*x.shape) for x in results] + [dma((4,)), dma((4,))],
        compiler_params=pltpu.CompilerParams(vmem_limit_bytes=60 * 1024 * 1024),
        name="drain",
    )(*results)


def solution(mesh):
    seq_head = P("seq", "head", None)
    rows = P(("seq", "head"), None)
    return jax.shard_map(
        functools.partial(per_device, mesh.shape["seq"]),
        mesh=mesh,
        in_specs=(seq_head, seq_head, seq_head, P("head", None), rows, P()),
        out_specs=(rows, seq_head, seq_head, seq_head),
        check_vma=False,
    )
```
